32 devices in a mesh: groups: 2 (over x), ctx: 16 (over z, y, core).
Axes of the slice: x: 2, y: 2, z: 4, core: 2. Of those that a mesh axis runs over, the one named last changes fastest.
Arguments:
- query_rows: bfloat16 [8192, 4096], P(('groups', 'ctx')), parts along dimension 0, may hold values from -6 to 6
- key_rows: bfloat16 [8192, 4096], P(('groups', 'ctx')), parts along dimension 0, may hold values from -6 to 6
- value_rows: bfloat16 [8192, 4096], P(('groups', 'ctx')), parts along dimension 0, may hold values from -45 to 45
- out_gain: float32 [4096], replicated, may hold values from 0.25 to 1.75
Outputs:
- attended: bfloat16 [8192, 4096], P(('groups', 'ctx')), parts along dimension 0
- final_state: float32 [8192, 128], P(('groups', 'ctx')), parts along dimension 0
The draws below stay inside these ranges and needn't reach their ends.
There are 2 independent parts, one for each index of `groups`. The reference program is written for one: setup_inputs(seed, part) draws one part's arguments, and reference() takes and returns one part's arrays. A program takes and returns all parts, laid end to end along the dimension named above; an argument that names none is the same for every part. Nothing has to cross between parts.
All inputs are finite; a program needn't handle non-finite values.
Results may differ from the reference program's by a relative error of at most 0.0051.
Values sent between devices are 32-bit elements; how exact they have to be, the bound alone decides.
A program may use at most 320 MiB of HBM per device.

```python
import math
import jax
import jax.numpy as jnp
from jax import lax

H = 32
DH = 128
BLK = 128
SEQ = 4096
FEAT = 4096


def draw_value_rows(key, part):
    key_rows, key_cols, key_base = jax.random.split(key, 3)
    low = math.log(0.3)
    high = math.log(3.0)
    row_scale = jnp.exp(jax.random.uniform(key_rows, (SEQ, 1), jnp.float32, low, high))
    col_scale = jnp.exp(jax.random.uniform(key_cols, (1, FEAT), jnp.float32, low, high))
    base = jax.random.normal(key_base, (SEQ, FEAT), jnp.float32)
    base = jnp.clip(base, -5.0, 5.0)
    return (base * row_scale * col_scale).astype(jnp.bfloat16)


def block_levels(key, shape, cuts, least, top_value):
    def one(position, parts):
        steps = jax.random.uniform(jax.random.fold_in(jax.random.fold_in(key, 6), position), (parts,), jnp.float32, least / len(cuts), top_value / len(cuts))
        return jnp.repeat(jnp.exp(steps), shape[position] // parts).reshape((-1,) + (1,) * (len(shape) - position - 1))

    factor_of = one(*cuts[0])
    for cut in cuts[1:]:
        factor_of = factor_of * one(*cut)
    return factor_of


def gaussian(stream_key, extent, width, reach, shards=(), kind=jnp.bfloat16):
    entries = jax.random.normal(stream_key, extent, jnp.float32) * width
    if len(shards) > 0:
        entries = block_levels(stream_key, extent, shards, -0.22, 0.18) * entries
    return jnp.clip(entries, min=-reach, max=reach).astype(kind)


def setup_inputs(seed: int = 0, part: int = 0) -> dict:
    streams_of = jax.random.split(jax.random.key(seed), 5)
    own_keys = jax.random.split(jax.random.fold_in(streams_of[4], part), 5)
    return {
        "query_rows": gaussian(own_keys[0], (SEQ, FEAT), 1.0, 6.0, ((0, 16),)),
        "key_rows": gaussian(own_keys[1], (SEQ, FEAT), 1.0, 6.0, ((0, 16),)),
        "value_rows": draw_value_rows(jax.random.fold_in(jax.random.fold_in(streams_of[4], part), 71), part),
        "out_gain": jnp.clip(1.0 + 0.15 * jax.random.normal(streams_of[3], (FEAT,), jnp.float32), 0.25, 1.75),
    }


def silu_round(values):
    return jax.nn.silu(values.astype(jnp.float32)).astype(jnp.bfloat16)

def rounded(values):
    return lax.optimization_barrier(values.astype(jnp.bfloat16)).astype(jnp.float32)

def reference(query_rows, key_rows, value_rows, out_gain):
    feat_q = silu_round(query_rows).reshape(-1, BLK, H, DH)
    feat_k = silu_round(key_rows).reshape(-1, BLK, H, DH)
    values = value_rows.reshape(-1, BLK, H, DH)
    causal = jnp.arange(BLK)[:, None] >= jnp.arange(BLK)[None, :]

    def advance(carried, block):
        q_blk, k_blk, v_blk = block
        q_f = q_blk.astype(jnp.float32)
        k_f = k_blk.astype(jnp.float32)
        v_f = v_blk.astype(jnp.float32)
        scores = jnp.einsum('ihd,jhd->hij', q_f, k_f)
        scores = rounded(jnp.where(causal[None], scores, jnp.float32(0.0)))
        intra = jnp.einsum('hij,jhd->ihd', scores, v_f)
        inter = jnp.einsum('ihd,hde->ihe', q_f, rounded(carried))
        state = jnp.einsum('jhd,jhe->hde', k_f, v_f)
        return (carried + state, intra + inter)
    start = jnp.zeros((H, DH, DH), jnp.float32)
    final, mixed = lax.scan(advance, start, (feat_q, feat_k, values))
    mixed = mixed.reshape(-1, H * DH)
    scale = lax.rsqrt(lax.optimization_barrier(jnp.mean(mixed * mixed, axis=1, keepdims=True)) + 1e-05)
    attended = (mixed * scale * out_gain[None, :]).astype(jnp.bfloat16)
    final_state = final.reshape(H * DH, DH) * SEQ ** (-0.5)
    return (attended, final_state)
```

```python
import functools

import jax
import jax.numpy as jnp
from jax import lax
from jax.experimental import pallas as pl
from jax.experimental.pallas import tpu as pltpu
from jax.sharding import PartitionSpec as P

H = 32
DH = 128
BLK = 128
FEAT = H * DH
F32 = jnp.float32
BF16 = jnp.bfloat16
MESH = pl.DeviceIdType.MESH


def silu_round(values):
    half = values.astype(F32) * 0.5
    return (half + half * jnp.tanh(half)).astype(BF16)


def kernel(n, q_hbm, k_hbm, v_hbm, gain_ref, out_ref, fs_ref,
           q_buf, k_buf, v_buf, scores, mixed, sumsq,
           total, first, prefix, x_in, chip, y_in, p_in, p_out, c_out, d_in, d_out,
           q_sem, k_sem, v_sem, x_snd, x_rcv, y_snd, y_rcv, p_snd, p_rcv,
           c_snd, c_rcv, d_snd, d_rcv):
    nz = n // 4
    rows = FEAT // n
    grain = min(rows, DH)
    subs = rows // grain
    steps = n // 2
    heads = 2 * rows // DH
    width = heads * DH
    me = lax.axis_index("ctx")
    grp = lax.axis_index("groups")
    z, y, c = me // 4, (me // 2) % 2, me % 2
    other_core = (grp, me + 1 - 2 * c)
    other_y = (grp, me + 2 - 4 * y)
    above = (grp, me + 4)
    below = (grp, me - 4)
    has_above = z < nz - 1
    has_below = z > 0

    def fetch(hbm, buf, sem, step):
        cols = pl.ds(pl.multiple_of(step * width, width), width)
        return pltpu.make_async_copy(hbm.at[:, cols], buf.at[:, cols], sem.at[step])

    def start_kv(step, _):
        fetch(k_hbm, k_buf, k_sem, step).start()
        fetch(v_hbm, v_buf, v_sem, step).start()
        return 0

    def start_q(step, _):
        fetch(q_hbm, q_buf, q_sem, step).start()
        return 0

    barrier = pltpu.get_barrier_semaphore()
    pl.semaphore_signal(barrier, inc=1, device_id=other_core, device_id_type=MESH)
    pl.semaphore_signal(barrier, inc=1, device_id=other_y, device_id_type=MESH)

    @pl.when(has_above)
    def _():
        pl.semaphore_signal(barrier, inc=1, device_id=above, device_id_type=MESH)

    @pl.when(has_below)
    def _():
        pl.semaphore_signal(barrier, inc=1, device_id=below, device_id_type=MESH)

    lax.fori_loop(0, steps, start_kv, 0)
    lax.fori_loop(0, steps, start_q, 0)

    sumsq[...] = jnp.zeros_like(sumsq)

    @pl.when(z == 0)
    def _():
        p_in[...] = jnp.zeros_like(p_in)

    @pl.when(z == nz - 1)
    def _():
        d_in[...] = jnp.zeros_like(d_in)

    neighbours = 2 + has_above.astype(jnp.int32) + has_below.astype(jnp.int32)
    pl.semaphore_wait(barrier, neighbours)

    def state_rows(step, core, sub):
        return pl.ds(pl.multiple_of((2 * step + core) * rows + sub * grain, grain), grain)

    def half_rows(j):
        return pl.ds(pl.multiple_of(j * grain, grain), grain)

    def remote(src, dst, snd, rcv, device):
        return pltpu.make_async_remote_copy(
            src_ref=src, dst_ref=dst, send_sem=snd, recv_sem=rcv,
            device_id=device, device_id_type=MESH)

    def x_copy(step, sub):
        j = step * subs + sub
        return remote(total.at[state_rows(step, 1 - c, sub)], x_in.at[half_rows(j)],
                      x_snd.at[j], x_rcv.at[j], other_core)

    def y_copy(j):
        return remote(chip.at[half_rows(j)], y_in.at[half_rows(j)],
                      y_snd.at[j], y_rcv.at[j], other_y)

    def p_copy(j):
        return remote(p_out.at[half_rows(j)], p_in.at[half_rows(j)],
                      p_snd.at[j], p_rcv.at[j], above)

    def c_copy(step, sub, core):
        j = step * subs + sub
        return remote(c_out.at[half_rows(j)], prefix.at[state_rows(step, core, sub)],
                      c_snd.at[j], c_rcv.at[j], other_core)

    def d_copy(i):
        return remote(d_out.at[half_rows(i)], d_in.at[half_rows(i)],
                      d_snd.at[i], d_rcv.at[i], below)

    def send_chip(step):
        for sub in range(subs):
            j = step * subs + sub
            x_copy(step, sub).wait_recv()
            chip[half_rows(j), :] = total[state_rows(step, c, sub), :] + x_in[half_rows(j), :]
            y_copy(j).start()

    def states(step, _):
        fetch(k_hbm, k_buf, k_sem, step).wait()
        fetch(v_hbm, v_buf, v_sem, step).wait()
        for a in range(heads):
            head = step * heads + a
            cols = pl.ds(pl.multiple_of(head * DH, DH), DH)
            feat = silu_round(k_buf[:, cols])
            k_buf[:, cols] = feat
            vals = v_buf[:, cols]
            parts = [
                lax.dot_general(feat[b * BLK:(b + 1) * BLK], vals[b * BLK:(b + 1) * BLK],
                                (((0,), (0,)), ((), ())), preferred_element_type=F32)
                for b in range(2)
            ]
            first[cols, :] = parts[0]
            total[cols, :] = parts[0] + parts[1]
        for sub in range(subs):
            x_copy(step, sub).start()

        @pl.when(step > 0)
        def _():
            send_chip(step - 1)

        return 0

    lax.fori_loop(0, steps, states, 0)
    send_chip(steps - 1)

    yf = y.astype(F32)
    cf = c.astype(F32)
    causal = (lax.broadcasted_iota(jnp.int32, (BLK, BLK), 0)
              >= lax.broadcasted_iota(jnp.int32, (BLK, BLK), 1))
    lag = (nz - 1 - z) * 4

    def pass_down(step):
        @pl.when((step >= 0) & (step % 2 == y) & (step // 2 < z))
        def _():
            for sub in range(subs):
                i = (step // 2) * subs + sub
                j = step * subs + sub

                @pl.when(has_above)
                def _():
                    d_copy(i).wait_recv()

                d_out[half_rows(i), :] = (d_in[half_rows(i), :] + chip[half_rows(j), :]
                                          + y_in[half_rows(j), :])
                d_copy(i).start()

    def finish(step):
        for sub in range(subs):
            c_copy(step, sub, 1 - c).wait_recv()
        acc = sumsq[...]
        outs = []
        for a in range(heads):
            head = step * heads + a
            cols = pl.ds(pl.multiple_of(head * DH, DH), DH)
            before = prefix[cols, :]
            carried = [before.astype(BF16), (before + first[cols, :]).astype(BF16)]
            blocks = []
            for b in range(2):
                toks = slice(b * BLK, (b + 1) * BLK)
                left = jnp.concatenate([scores[toks, cols], q_buf[toks, cols]], axis=1)
                right = jnp.concatenate([v_buf[toks, cols], carried[b]], axis=0)
                blocks.append(jnp.dot(left, right, preferred_element_type=F32))
            both = jnp.concatenate(blocks, axis=0)
            mixed[:, cols] = both
            acc = acc + both * both
        sumsq[...] = acc

    def carry(step, _):
        for sub in range(subs):
            j = step * subs + sub
            here = half_rows(j)
            y_copy(j).wait_recv()

            @pl.when(has_below)
            def _():
                p_copy(j).wait_recv()

            arrived = p_in[here, :]
            sibling = y_in[here, :]
            p_out[here, :] = arrived + chip[here, :] + sibling

            @pl.when(has_above)
            def _():
                p_copy(j).start()

            base = arrived + yf * sibling
            mine = state_rows(step, c, sub)
            c_out[here, :] = base + (1.0 - cf) * total[mine, :]
            c_copy(step, sub, c).start()
            prefix[mine, :] = base + cf * x_in[here, :]
        pass_down(step - lag)
        fetch(q_hbm, q_buf, q_sem, step).wait()
        for a in range(heads):
            head = step * heads + a
            cols = pl.ds(pl.multiple_of(head * DH, DH), DH)
            feat = silu_round(q_buf[:, cols])
            q_buf[:, cols] = feat
            for b in range(2):
                toks = slice(b * BLK, (b + 1) * BLK)
                s = lax.dot_general(feat[toks], k_buf[toks, cols],
                                    (((1,), (1,)), ((), ())), preferred_element_type=F32)
                scores[toks, cols] = jnp.where(causal, s, 0.0).astype(BF16)

        @pl.when(step > 0)
        def _():
            finish(step - 1)

        return 0

    lax.fori_loop(0, steps, carry, 0)

    def rest_down(step, _):
        @pl.when(step + lag >= steps)
        def _():
            pass_down(step)

        return 0

    lax.fori_loop(0, steps, rest_down, 0)
    finish(steps - 1)

    scale = lax.rsqrt(jnp.sum(sumsq[...], axis=1, keepdims=True) * (1.0 / FEAT) + 1e-05)

    def normalize(step, _):
        cols = pl.ds(pl.multiple_of(step * width, width), width)
        out_ref[:, cols] = (mixed[:, cols] * scale * gain_ref[:, cols]).astype(BF16)
        return 0

    lax.fori_loop(0, steps, normalize, 0)

    for sub in range(subs):
        @pl.when(has_above)
        def _():
            d_copy(z * subs + sub).wait_recv()

        j = (2 * z + y) * subs + sub
        fs_ref[sub * grain:(sub + 1) * grain, :] = (
            p_out[half_rows(j), :] + d_in[half_rows(z * subs + sub), :]) * (
                (n * q_buf.shape[0]) ** -0.5)

    def drain(step, _):
        for sub in range(subs):
            j = step * subs + sub
            x_copy(step, sub).wait_send()
            y_copy(j).wait_send()

            @pl.when(has_above)
            def _():
                p_copy(j).wait_send()

            c_copy(step, sub, c).wait_send()
        return 0

    lax.fori_loop(0, steps, drain, 0)

    def drain_down(i, _):
        d_copy(i).wait_send()
        return 0

    lax.fori_loop(0, z * subs, drain_down, 0)


def shards(n, query_rows, key_rows, value_rows, out_gain):
    toks = query_rows.shape[0]
    rows = FEAT // n
    grain = min(rows, DH)
    chunks = FEAT // 2 // grain
    downs = (n // 4) * (rows // grain)
    steps = n // 2
    full = pltpu.VMEM((FEAT, DH), F32)
    half = pltpu.VMEM((FEAT // 2, DH), F32)
    down = pltpu.VMEM((downs * grain, DH), F32)
    wide = pltpu.VMEM((toks, FEAT), BF16)
    dma = pltpu.SemaphoreType.DMA
    return pl.pallas_call(
        functools.partial(kernel, n),
        out_shape=(jax.ShapeDtypeStruct((toks, FEAT), BF16),
                   jax.ShapeDtypeStruct((rows, DH), F32)),
        in_specs=[pl.BlockSpec(memory_space=pl.ANY)] * 3
        + [pl.BlockSpec(memory_space=pltpu.VMEM)],
        out_specs=(pl.BlockSpec(memory_space=pltpu.VMEM),
                   pl.BlockSpec(memory_space=pltpu.VMEM)),
        scratch_shapes=[wide] * 4 + [pltpu.VMEM((toks, FEAT), F32), pltpu.VMEM((toks, DH), F32)]
        + [full] * 3 + [half] * 6 + [down] * 2
        + [dma((steps,))] * 3 + [dma((chunks,))] * 8 + [dma((downs,))] * 2,
        compiler_params=pltpu.CompilerParams(
            collective_id=0, has_side_effects=True, vmem_limit_bytes=56 * 1024 * 1024),
        cost_estimate=pl.CostEstimate(
            flops=2 * 4 * toks * FEAT * DH, bytes_accessed=8 * toks * FEAT,
            transcendentals=2 * toks * FEAT),
    )(query_rows, key_rows, value_rows, out_gain.reshape(1, FEAT))


def solution(mesh):
    rows = P(("groups", "ctx"), None)
    return jax.shard_map(
        functools.partial(shards, mesh.shape["ctx"]),
        mesh=mesh,
        in_specs=(rows, rows, rows, P()),
        out_specs=(rows, rows),
        check_vma=False,
    )
```

```python
import functools

import jax
import jax.numpy as jnp
from jax import lax
from jax.experimental import pallas as pl
from jax.experimental.pallas import tpu as pltpu
from jax.sharding import PartitionSpec as P

H = 32
DH = 128
BLK = 128
FEAT = H * DH
F32 = jnp.float32
BF16 = jnp.bfloat16
MESH = pl.DeviceIdType.MESH
BEHIND = 2


def silu_round(values):
    half = values.astype(F32) * 0.5
    return (half + half * jnp.tanh(half)).astype(BF16)


def kernel(n, q_hbm, k_hbm, v_hbm, gain_ref, out_ref, fs_ref,
           q_buf, k_buf, v_buf, scores, mixed, sumsq,
           total, first, prefix, x_in, chip, c_out,
           e_in, p_in, p_out, r_in, r_out, d_in, d_out,
           q_sem, k_sem, v_sem, x_snd, x_rcv, c_snd, c_rcv,
           e_snd, e_rcv, p_snd, p_rcv, r_snd, r_rcv, d_snd, d_rcv):
    nz = n // 4
    rows = FEAT // n
    grain = min(rows, DH)
    subs = rows // grain
    steps = n // 2
    heads = 2 * rows // DH
    width = heads * DH
    me = lax.axis_index("ctx")
    grp = lax.axis_index("groups")
    z, y, c = me // 4, (me // 2) % 2, me % 2
    other_core = (grp, me + 1 - 2 * c)
    other_y = (grp, me + 2 - 4 * y)
    above = (grp, me + 4)
    below = (grp, me - 4)
    has_above = z < nz - 1
    has_below = z > 0

    def fetch(hbm, buf, sem, step):
        cols = pl.ds(pl.multiple_of(step * width, width), width)
        return pltpu.make_async_copy(hbm.at[:, cols], buf.at[:, cols], sem.at[step])

    def start_kv(step, _):
        fetch(k_hbm, k_buf, k_sem, step).start()
        fetch(v_hbm, v_buf, v_sem, step).start()
        return 0

    def start_q(step, _):
        fetch(q_hbm, q_buf, q_sem, step).start()
        return 0

    barrier = pltpu.get_barrier_semaphore()
    pl.semaphore_signal(barrier, inc=1, device_id=other_core, device_id_type=MESH)
    pl.semaphore_signal(barrier, inc=1, device_id=other_y, device_id_type=MESH)

    @pl.when(has_above)
    def _():
        pl.semaphore_signal(barrier, inc=1, device_id=above, device_id_type=MESH)

    @pl.when(has_below)
    def _():
        pl.semaphore_signal(barrier, inc=1, device_id=below, device_id_type=MESH)

    lax.fori_loop(0, steps, start_kv, 0)
    lax.fori_loop(0, steps, start_q, 0)

    sumsq[...] = jnp.zeros_like(sumsq)

    @pl.when(z == 0)
    def _():
        p_in[...] = jnp.zeros_like(p_in)

    @pl.when(z == nz - 1)
    def _():
        d_in[...] = jnp.zeros_like(d_in)

    neighbours = 2 + has_above.astype(jnp.int32) + has_below.astype(jnp.int32)
    pl.semaphore_wait(barrier, neighbours)

    def state_rows(piece, core, sub):
        return pl.ds(pl.multiple_of((2 * piece + core) * rows + sub * grain, grain), grain)

    def chunk(j):
        return pl.ds(pl.multiple_of(j * grain, grain), grain)

    def remote(src, dst, snd, rcv, device):
        return pltpu.make_async_remote_copy(
            src_ref=src, dst_ref=dst, send_sem=snd, recv_sem=rcv,
            device_id=device, device_id_type=MESH)

    def x_copy(piece, sub):
        j = piece * subs + sub
        return remote(total.at[state_rows(piece, 1 - c, sub)], x_in.at[chunk(j)],
                      x_snd.at[j], x_rcv.at[j], other_core)

    def e_copy(i):
        j = half_index(i, 1 - y)
        return remote(chip.at[chunk(j)], e_in.at[chunk(i)], e_snd.at[i], e_rcv.at[i], other_y)

    def p_copy(i):
        return remote(p_out.at[chunk(i)], p_in.at[chunk(i)], p_snd.at[i], p_rcv.at[i], above)

    def r_copy(i):
        return remote(r_out.at[chunk(i)], r_in.at[chunk(i)], r_snd.at[i], r_rcv.at[i], other_y)

    def c_copy(i, yy, core):
        j = half_index(i, yy)
        return remote(c_out.at[chunk(j)],
                      prefix.at[state_rows(2 * (i // subs) + yy, core, i % subs)],
                      c_snd.at[j], c_rcv.at[j], other_core)

    def d_copy(i):
        return remote(d_out.at[chunk(i)], d_in.at[chunk(i)], d_snd.at[i], d_rcv.at[i], below)

    def half_index(i, yy):
        return (2 * (i // subs) + yy) * subs + i % subs

    def send_chip(piece):
        for sub in range(subs):
            j = piece * subs + sub
            x_copy(piece, sub).wait_recv()
            chip[chunk(j), :] = total[state_rows(piece, c, sub), :] + x_in[chunk(j), :]

            @pl.when(piece % 2 != y)
            def _():
                e_copy((piece // 2) * subs + sub).start()

    def states(step, _):
        fetch(k_hbm, k_buf, k_sem, step).wait()
        fetch(v_hbm, v_buf, v_sem, step).wait()
        for a in range(heads):
            head = step * heads + a
            cols = pl.ds(pl.multiple_of(head * DH, DH), DH)
            feat = silu_round(k_buf[:, cols])
            k_buf[:, cols] = feat
            vals = v_buf[:, cols]
            parts = [
                lax.dot_general(feat[b * BLK:(b + 1) * BLK], vals[b * BLK:(b + 1) * BLK],
                                (((0,), (0,)), ((), ())), preferred_element_type=F32)
                for b in range(2)
            ]
            first[cols, :] = parts[0]
            total[cols, :] = parts[0] + parts[1]
        for sub in range(subs):
            x_copy(step, sub).start()

        @pl.when(step > 0)
        def _():
            send_chip(step - 1)

        return 0

    lax.fori_loop(0, steps, states, 0)
    send_chip(steps - 1)

    yf = y.astype(F32)
    cf = c.astype(F32)
    causal = (lax.broadcasted_iota(jnp.int32, (BLK, BLK), 0)
              >= lax.broadcasted_iota(jnp.int32, (BLK, BLK), 1))
    count = nz * subs
    lag = (nz - 1 - z) * 4

    def heads_of(i, yy):
        piece = 2 * (i // subs) + yy
        if rows < DH:
            return [piece]
        return [(2 * piece + core) * subs + i % subs for core in range(2)]

    def head_cols(head):
        return pl.ds(pl.multiple_of(head * DH, DH), DH)

    def pass_down(i):
        @pl.when((i >= 0) & (i // subs < z))
        def _():
            @pl.when(has_above)
            def _():
                d_copy(i).wait_recv()

            d_out[chunk(i), :] = (d_in[chunk(i), :] + chip[chunk(half_index(i, y)), :]
                                  + e_in[chunk(i), :])
            d_copy(i).start()

    def share(i, yy, base):
        j = half_index(i, yy)
        mine = state_rows(2 * (i // subs) + yy, c, i % subs)
        c_out[chunk(j), :] = base + (1.0 - cf) * total[mine, :]
        c_copy(i, yy, c).start()
        prefix[mine, :] = base + cf * x_in[chunk(j), :]

    def finish(i, yy):
        c_copy(i, yy, 1 - c).wait_recv()
        acc = sumsq[...]
        for head in heads_of(i, yy):
            cols = head_cols(head)
            before = prefix[cols, :]
            carried = [before.astype(BF16), (before + first[cols, :]).astype(BF16)]
            blocks = []
            for b in range(2):
                toks = slice(b * BLK, (b + 1) * BLK)
                left = jnp.concatenate([scores[toks, cols], q_buf[toks, cols]], axis=1)
                right = jnp.concatenate([v_buf[toks, cols], carried[b]], axis=0)
                blocks.append(jnp.dot(left, right, preferred_element_type=F32))
            both = jnp.concatenate(blocks, axis=0)
            mixed[:, cols] = both
            acc = acc + both * both
        sumsq[...] = acc

    def score(i):
        for yy in range(2):
            for head in heads_of(i, yy):
                cols = head_cols(head)
                feat = silu_round(q_buf[:, cols])
                q_buf[:, cols] = feat
                for b in range(2):
                    toks = slice(b * BLK, (b + 1) * BLK)
                    s = lax.dot_general(feat[toks], k_buf[toks, cols],
                                        (((1,), (1,)), ((), ())), preferred_element_type=F32)
                    scores[toks, cols] = jnp.where(causal, s, 0.0).astype(BF16)

    def carry(i, _):
        @pl.when(i < count)
        def _():
            here = chunk(i)
            e_copy(i).wait_recv()

            @pl.when(has_below)
            def _():
                p_copy(i).wait_recv()

            arrived = p_in[here, :]
            sibling = e_in[here, :]
            own = chip[chunk(half_index(i, y)), :]
            p_out[here, :] = arrived + own + sibling

            @pl.when(has_above)
            def _():
                p_copy(i).start()

            r_out[here, :] = arrived + (1.0 - yf) * own
            r_copy(i).start()
            share(i, y, arrived + yf * sibling)

        back = i - BEHIND

        @pl.when((back >= 0) & (back < count))
        def _():
            r_copy(back).wait_recv()
            share(back, 1 - y, r_in[chunk(back), :])

        @pl.when(i - lag < count)
        def _():
            pass_down(i - lag)

        @pl.when(i < count)
        def _():
            @pl.when(i % subs == 0)
            def _():
                for piece in range(2):
                    fetch(q_hbm, q_buf, q_sem, 2 * (i // subs) + piece).wait()
            score(i)

        @pl.when((i >= 1) & (i - 1 < count))
        def _():
            finish(i - 1, y)

        @pl.when(back >= 1)
        def _():
            finish(back - 1, 1 - y)

        return 0

    trips = count + BEHIND + 1
    lax.fori_loop(0, trips, carry, 0)

    def rest_down(i, _):
        @pl.when(i + lag >= trips)
        def _():
            pass_down(i)

        return 0

    lax.fori_loop(0, count, rest_down, 0)

    scale = lax.rsqrt(jnp.sum(sumsq[...], axis=1, keepdims=True) * (1.0 / FEAT) + 1e-05)

    def normalize(step, _):
        cols = pl.ds(pl.multiple_of(step * width, width), width)
        out_ref[:, cols] = (mixed[:, cols] * scale * gain_ref[:, cols]).astype(BF16)
        return 0

    lax.fori_loop(0, steps, normalize, 0)

    for sub in range(subs):
        i = z * subs + sub

        @pl.when(has_above)
        def _():
            d_copy(i).wait_recv()

        fs_ref[sub * grain:(sub + 1) * grain, :] = (
            p_out[chunk(i), :] + d_in[chunk(i), :]) * ((n * q_buf.shape[0]) ** -0.5)

    def drain(i, _):
        for piece in range(2):
            x_copy(2 * (i // subs) + piece, i % subs).wait_send()
            c_copy(i, piece, c).wait_send()
        e_copy(i).wait_send()
        r_copy(i).wait_send()

        @pl.when(has_above)
        def _():
            p_copy(i).wait_send()

        @pl.when(i // subs < z)
        def _():
            d_copy(i).wait_send()

        return 0

    lax.fori_loop(0, count, drain, 0)


def shards(n, query_rows, key_rows, value_rows, out_gain):
    toks = query_rows.shape[0]
    rows = FEAT // n
    grain = min(rows, DH)
    chunks = FEAT // 2 // grain
    steps = n // 2
    full = pltpu.VMEM((FEAT, DH), F32)
    half = pltpu.VMEM((FEAT // 2, DH), F32)
    quarter = pltpu.VMEM((FEAT // 4, DH), F32)
    wide = pltpu.VMEM((toks, FEAT), BF16)
    dma = pltpu.SemaphoreType.DMA
    return pl.pallas_call(
        functools.partial(kernel, n),
        out_shape=(jax.ShapeDtypeStruct((toks, FEAT), BF16),
                   jax.ShapeDtypeStruct((rows, DH), F32)),
        in_specs=[pl.BlockSpec(memory_space=pl.ANY)] * 3
        + [pl.BlockSpec(memory_space=pltpu.VMEM)],
        out_specs=(pl.BlockSpec(memory_space=pltpu.VMEM),
                   pl.BlockSpec(memory_space=pltpu.VMEM)),
        scratch_shapes=[wide] * 4 + [pltpu.VMEM((toks, FEAT), F32), pltpu.VMEM((toks, DH), F32)]
        + [full] * 3 + [half] * 3 + [quarter] * 7
        + [dma((steps,))] * 3 + [dma((chunks,))] * 4 + [dma((chunks // 2,))] * 8,
        compiler_params=pltpu.CompilerParams(
            collective_id=0, has_side_effects=True, vmem_limit_bytes=56 * 1024 * 1024),
        cost_estimate=pl.CostEstimate(
            flops=2 * 4 * toks * FEAT * DH, bytes_accessed=8 * toks * FEAT,
            transcendentals=2 * toks * FEAT),
    )(query_rows, key_rows, value_rows, out_gain.reshape(1, FEAT))


def solution(mesh):
    rows = P(("groups", "ctx"), None)
    return jax.shard_map(
        functools.partial(shards, mesh.shape["ctx"]),
        mesh=mesh,
        in_specs=(rows, rows, rows, P()),
        out_specs=(rows, rows),
        check_vma=False,
    )
```

```python
import functools

import jax
import jax.numpy as jnp
from jax import lax
from jax.experimental import pallas as pl
from jax.experimental.pallas import tpu as pltpu
from jax.sharding import PartitionSpec as P

H = 32
DH = 128
BLK = 128
FEAT = H * DH
F32 = jnp.float32
BF16 = jnp.bfloat16
MESH = pl.DeviceIdType.MESH
BEHIND = 3
SLACK = 2


def silu_round(values):
    half = values.astype(F32) * 0.5
    return (half + half * jnp.tanh(half)).astype(BF16)


def kernel(n, q_hbm, k_hbm, v_hbm, gain_ref, out_ref, fs_ref,
           q_buf, k_buf, v_buf, scores, mixed, sumsq,
           total, first, prefix, x_in, chip, c_out,
           e_in, p_in, p_out, r_in, r_out, d_in, d_out,
           q_sem, k_sem, v_sem, x_snd, x_rcv, c_snd, c_rcv,
           e_snd, e_rcv, p_snd, p_rcv, r_snd, r_rcv, d_snd, d_rcv):
    nz = n // 4
    rows = FEAT // n
    grain = min(rows, DH)
    subs = rows // grain
    steps = n // 2
    heads = 2 * rows // DH
    width = heads * DH
    me = lax.axis_index("ctx")
    grp = lax.axis_index("groups")
    z, y, c = me // 4, (me // 2) % 2, me % 2
    other_core = (grp, me + 1 - 2 * c)
    other_y = (grp, me + 2 - 4 * y)
    above = (grp, me + 4)
    below = (grp, me - 4)
    has_above = z < nz - 1
    has_below = z > 0

    def fetch(hbm, buf, sem, step):
        cols = pl.ds(pl.multiple_of(step * width, width), width)
        return pltpu.make_async_copy(hbm.at[:, cols], buf.at[:, cols], sem.at[step])

    def start_kv(step, _):
        fetch(k_hbm, k_buf, k_sem, step).start()
        fetch(v_hbm, v_buf, v_sem, step).start()
        return 0

    def start_q(step, _):
        fetch(q_hbm, q_buf, q_sem, step).start()
        return 0

    barrier = pltpu.get_barrier_semaphore()
    pl.semaphore_signal(barrier, inc=1, device_id=other_core, device_id_type=MESH)
    pl.semaphore_signal(barrier, inc=1, device_id=other_y, device_id_type=MESH)

    @pl.when(has_above)
    def _():
        pl.semaphore_signal(barrier, inc=1, device_id=above, device_id_type=MESH)

    @pl.when(has_below)
    def _():
        pl.semaphore_signal(barrier, inc=1, device_id=below, device_id_type=MESH)

    lax.fori_loop(0, steps, start_kv, 0)
    lax.fori_loop(0, steps, start_q, 0)

    sumsq[...] = jnp.zeros_like(sumsq)

    @pl.when(z == 0)
    def _():
        p_in[...] = jnp.zeros_like(p_in)

    @pl.when(z == nz - 1)
    def _():
        d_in[...] = jnp.zeros_like(d_in)

    neighbours = 2 + has_above.astype(jnp.int32) + has_below.astype(jnp.int32)
    pl.semaphore_wait(barrier, neighbours)

    def state_rows(piece, core, sub):
        return pl.ds(pl.multiple_of((2 * piece + core) * rows + sub * grain, grain), grain)

    def chunk(j):
        return pl.ds(pl.multiple_of(j * grain, grain), grain)

    def remote(src, dst, snd, rcv, device):
        return pltpu.make_async_remote_copy(
            src_ref=src, dst_ref=dst, send_sem=snd, recv_sem=rcv,
            device_id=device, device_id_type=MESH)

    def x_copy(piece, sub):
        j = piece * subs + sub
        return remote(total.at[state_rows(piece, 1 - c, sub)], x_in.at[chunk(j)],
                      x_snd.at[j], x_rcv.at[j], other_core)

    def e_copy(i):
        j = half_index(i, 1 - y)
        return remote(chip.at[chunk(j)], e_in.at[chunk(i)], e_snd.at[i], e_rcv.at[i], other_y)

    def p_copy(i):
        return remote(p_out.at[chunk(i)], p_in.at[chunk(i)], p_snd.at[i], p_rcv.at[i], above)

    def r_copy(i):
        return remote(r_out.at[chunk(i)], r_in.at[chunk(i)], r_snd.at[i], r_rcv.at[i], other_y)

    def c_copy(i, yy, core):
        j = half_index(i, yy)
        return remote(c_out.at[chunk(j)],
                      prefix.at[state_rows(2 * (i // subs) + yy, core, i % subs)],
                      c_snd.at[j], c_rcv.at[j], other_core)

    def d_copy(i):
        return remote(d_out.at[chunk(i)], d_in.at[chunk(i)], d_snd.at[i], d_rcv.at[i], below)

    def half_index(i, yy):
        return (2 * (i // subs) + yy) * subs + i % subs

    def send_chip(piece):
        for sub in range(subs):
            j = piece * subs + sub
            x_copy(piece, sub).wait_recv()
            chip[chunk(j), :] = total[state_rows(piece, c, sub), :] + x_in[chunk(j), :]

            @pl.when(piece % 2 != y)
            def _():
                e_copy((piece // 2) * subs + sub).start()

    def states(step, _):
        fetch(k_hbm, k_buf, k_sem, step).wait()
        fetch(v_hbm, v_buf, v_sem, step).wait()
        for a in range(heads):
            head = step * heads + a
            cols = pl.ds(pl.multiple_of(head * DH, DH), DH)
            feat = silu_round(k_buf[:, cols])
            k_buf[:, cols] = feat
            vals = v_buf[:, cols]
            parts = [
                lax.dot_general(feat[b * BLK:(b + 1) * BLK], vals[b * BLK:(b + 1) * BLK],
                                (((0,), (0,)), ((), ())), preferred_element_type=F32)
                for b in range(2)
            ]
            first[cols, :] = parts[0]
            total[cols, :] = parts[0] + parts[1]
        for sub in range(subs):
            x_copy(step, sub).start()

        @pl.when(step > 0)
        def _():
            send_chip(step - 1)

        return 0

    lax.fori_loop(0, steps, states, 0)
    send_chip(steps - 1)

    yf = y.astype(F32)
    cf = c.astype(F32)
    causal = (lax.broadcasted_iota(jnp.int32, (BLK, BLK), 0)
              >= lax.broadcasted_iota(jnp.int32, (BLK, BLK), 1))
    count = nz * subs
    lag = (nz - 1 - z) * 4
    behind = BEHIND + SLACK * (nz - 1 - z)

    def heads_of(i, yy):
        piece = 2 * (i // subs) + yy
        if rows < DH:
            return [piece]
        return [(2 * piece + core) * subs + i % subs for core in range(2)]

    def head_cols(head):
        return pl.ds(pl.multiple_of(head * DH, DH), DH)

    def pass_down(i):
        @pl.when((i >= 0) & (i // subs < z))
        def _():
            @pl.when(has_above)
            def _():
                d_copy(i).wait_recv()

            d_out[chunk(i), :] = (d_in[chunk(i), :] + chip[chunk(half_index(i, y)), :]
                                  + e_in[chunk(i), :])
            d_copy(i).start()

    def share(i, yy, base):
        j = half_index(i, yy)
        mine = state_rows(2 * (i // subs) + yy, c, i % subs)
        c_out[chunk(j), :] = base + (1.0 - cf) * total[mine, :]
        c_copy(i, yy, c).start()
        prefix[mine, :] = base + cf * x_in[chunk(j), :]

    def finish(i, yy):
        c_copy(i, yy, 1 - c).wait_recv()
        acc = sumsq[...]
        for head in heads_of(i, yy):
            cols = head_cols(head)
            before = prefix[cols, :]
            carried = [before.astype(BF16), (before + first[cols, :]).astype(BF16)]
            blocks = []
            for b in range(2):
                toks = slice(b * BLK, (b + 1) * BLK)
                left = jnp.concatenate([scores[toks, cols], q_buf[toks, cols]], axis=1)
                right = jnp.concatenate([v_buf[toks, cols], carried[b]], axis=0)
                blocks.append(jnp.dot(left, right, preferred_element_type=F32))
            both = jnp.concatenate(blocks, axis=0)
            mixed[:, cols] = both
            acc = acc + both * both
        sumsq[...] = acc

    def score(i):
        for yy in range(2):
            for head in heads_of(i, yy):
                cols = head_cols(head)
                feat = silu_round(q_buf[:, cols])
                q_buf[:, cols] = feat
                for b in range(2):
                    toks = slice(b * BLK, (b + 1) * BLK)
                    s = lax.dot_general(feat[toks], k_buf[toks, cols],
                                        (((1,), (1,)), ((), ())), preferred_element_type=F32)
                    scores[toks, cols] = jnp.where(causal, s, 0.0).astype(BF16)

    def carry(i, _):
        @pl.when(i < count)
        def _():
            here = chunk(i)
            e_copy(i).wait_recv()

            @pl.when(has_below)
            def _():
                p_copy(i).wait_recv()

            arrived = p_in[here, :]
            sibling = e_in[here, :]
            own = chip[chunk(half_index(i, y)), :]
            p_out[here, :] = arrived + own + sibling

            @pl.when(has_above)
            def _():
                p_copy(i).start()

            r_out[here, :] = arrived + (1.0 - yf) * own
            r_copy(i).start()
            share(i, y, arrived + yf * sibling)

        back = i - behind

        @pl.when((back >= 0) & (back < count))
        def _():
            r_copy(back).wait_recv()
            share(back, 1 - y, r_in[chunk(back), :])

        @pl.when(i - lag < count)
        def _():
            pass_down(i - lag)

        @pl.when(i < count)
        def _():
            @pl.when(i % subs == 0)
            def _():
                for piece in range(2):
                    fetch(q_hbm, q_buf, q_sem, 2 * (i // subs) + piece).wait()
            score(i)

        @pl.when((i >= 1) & (i - 1 < count))
        def _():
            finish(i - 1, y)

        @pl.when(back >= 1)
        def _():
            finish(back - 1, 1 - y)

        return 0

    trips = count + behind + 1
    lax.fori_loop(0, trips, carry, 0)

    def rest_down(i, _):
        @pl.when(i + lag >= trips)
        def _():
            pass_down(i)

        return 0

    lax.fori_loop(0, count, rest_down, 0)

    scale = lax.rsqrt(jnp.sum(sumsq[...], axis=1, keepdims=True) * (1.0 / FEAT) + 1e-05)

    def normalize(step, _):
        cols = pl.ds(pl.multiple_of(step * width, width), width)
        out_ref[:, cols] = (mixed[:, cols] * scale * gain_ref[:, cols]).astype(BF16)
        return 0

    lax.fori_loop(0, steps, normalize, 0)

    for sub in range(subs):
        i = z * subs + sub

        @pl.when(has_above)
        def _():
            d_copy(i).wait_recv()

        fs_ref[sub * grain:(sub + 1) * grain, :] = (
            p_out[chunk(i), :] + d_in[chunk(i), :]) * ((n * q_buf.shape[0]) ** -0.5)

    def drain(i, _):
        for piece in range(2):
            x_copy(2 * (i // subs) + piece, i % subs).wait_send()
            c_copy(i, piece, c).wait_send()
        e_copy(i).wait_send()
        r_copy(i).wait_send()

        @pl.when(has_above)
        def _():
            p_copy(i).wait_send()

        @pl.when(i // subs < z)
        def _():
            d_copy(i).wait_send()

        return 0

    lax.fori_loop(0, count, drain, 0)


def shards(n, query_rows, key_rows, value_rows, out_gain):
    toks = query_rows.shape[0]
    rows = FEAT // n
    grain = min(rows, DH)
    chunks = FEAT // 2 // grain
    steps = n // 2
    full = pltpu.VMEM((FEAT, DH), F32)
    half = pltpu.VMEM((FEAT // 2, DH), F32)
    quarter = pltpu.VMEM((FEAT // 4, DH), F32)
    wide = pltpu.VMEM((toks, FEAT), BF16)
    dma = pltpu.SemaphoreType.DMA
    return pl.pallas_call(
        functools.partial(kernel, n),
        out_shape=(jax.ShapeDtypeStruct((toks, FEAT), BF16),
                   jax.ShapeDtypeStruct((rows, DH), F32)),
        in_specs=[pl.BlockSpec(memory_space=pl.ANY)] * 3
        + [pl.BlockSpec(memory_space=pltpu.VMEM)],
        out_specs=(pl.BlockSpec(memory_space=pltpu.VMEM),
                   pl.BlockSpec(memory_space=pltpu.VMEM)),
        scratch_shapes=[wide] * 4 + [pltpu.VMEM((toks, FEAT), F32), pltpu.VMEM((toks, DH), F32)]
        + [full] * 3 + [half] * 3 + [quarter] * 7
        + [dma((steps,))] * 3 + [dma((chunks,))] * 4 + [dma((chunks // 2,))] * 8,
        compiler_params=pltpu.CompilerParams(
            collective_id=0, has_side_effects=True, vmem_limit_bytes=50 * 1024 * 1024),
        cost_estimate=pl.CostEstimate(
            flops=2 * 4 * toks * FEAT * DH, bytes_accessed=8 * toks * FEAT,
            transcendentals=2 * toks * FEAT),
    )(query_rows, key_rows, value_rows, out_gain.reshape(1, FEAT))


def solution(mesh):
    rows = P(("groups", "ctx"), None)
    return jax.shard_map(
        functools.partial(shards, mesh.shape["ctx"]),
        mesh=mesh,
        in_specs=(rows, rows, rows, P()),
        out_specs=(rows, rows),
        check_vma=False,
    )
```

```python
import functools

import jax
import jax.numpy as jnp
from jax import lax
from jax.experimental import pallas as pl
from jax.experimental.pallas import tpu as pltpu
from jax.sharding import PartitionSpec as P

H = 32
DH = 128
BLK = 128
FEAT = H * DH
F32 = jnp.float32
BF16 = jnp.bfloat16
MESH = pl.DeviceIdType.MESH
BEHIND = 4
SLACK = 2


def silu_round(values):
    half = values.astype(F32) * 0.5
    return (half + half * jnp.tanh(half)).astype(BF16)


def kernel(n, q_hbm, k_hbm, v_hbm, gain_ref, out_ref, fs_ref,
           q_buf, k_buf, v_buf, scores, mixed, sumsq,
           total, first, prefix, x_in, chip, c_out,
           e_in, p_in, p_out, r_in, r_out, d_in, d_out,
           q_sem, k_sem, v_sem, x_snd, x_rcv, c_snd, c_rcv,
           e_snd, e_rcv, p_snd, p_rcv, r_snd, r_rcv, d_snd, d_rcv):
    nz = n // 4
    rows = FEAT // n
    grain = min(rows, DH)
    subs = rows // grain
    steps = n // 2
    heads = 2 * rows // DH
    width = heads * DH
    me = lax.axis_index("ctx")
    grp = lax.axis_index("groups")
    z, y, c = me // 4, (me // 2) % 2, me % 2
    other_core = (grp, me + 1 - 2 * c)
    other_y = (grp, me + 2 - 4 * y)
    above = (grp, me + 4)
    below = (grp, me - 4)
    has_above = z < nz - 1
    has_below = z > 0

    def fetch(hbm, buf, sem, step):
        cols = pl.ds(pl.multiple_of(step * width, width), width)
        return pltpu.make_async_copy(hbm.at[:, cols], buf.at[:, cols], sem.at[step])

    def piece_at(step):
        return 2 * (step % nz) + jnp.where(step < nz, 1 - y, y)

    def start_kv(step, _):
        piece = piece_at(step)
        fetch(k_hbm, k_buf, k_sem, piece).start()
        fetch(v_hbm, v_buf, v_sem, piece).start()
        return 0

    def start_q(step, _):
        fetch(q_hbm, q_buf, q_sem, step).start()
        return 0

    barrier = pltpu.get_barrier_semaphore()
    pl.semaphore_signal(barrier, inc=1, device_id=other_core, device_id_type=MESH)
    pl.semaphore_signal(barrier, inc=1, device_id=other_y, device_id_type=MESH)

    @pl.when(has_above)
    def _():
        pl.semaphore_signal(barrier, inc=1, device_id=above, device_id_type=MESH)

    @pl.when(has_below)
    def _():
        pl.semaphore_signal(barrier, inc=1, device_id=below, device_id_type=MESH)

    lax.fori_loop(0, steps, start_kv, 0)
    lax.fori_loop(0, steps, start_q, 0)

    sumsq[...] = jnp.zeros_like(sumsq)

    @pl.when(z == 0)
    def _():
        p_in[...] = jnp.zeros_like(p_in)

    @pl.when(z == nz - 1)
    def _():
        d_in[...] = jnp.zeros_like(d_in)

    neighbours = 2 + has_above.astype(jnp.int32) + has_below.astype(jnp.int32)

    def state_rows(piece, core, sub):
        return pl.ds(pl.multiple_of((2 * piece + core) * rows + sub * grain, grain), grain)

    def chunk(j):
        return pl.ds(pl.multiple_of(j * grain, grain), grain)

    def remote(src, dst, snd, rcv, device):
        return pltpu.make_async_remote_copy(
            src_ref=src, dst_ref=dst, send_sem=snd, recv_sem=rcv,
            device_id=device, device_id_type=MESH)

    def x_copy(piece, sub):
        j = piece * subs + sub
        return remote(total.at[state_rows(piece, 1 - c, sub)], x_in.at[chunk(j)],
                      x_snd.at[j], x_rcv.at[j], other_core)

    def e_copy(i):
        j = half_index(i, 1 - y)
        return remote(chip.at[chunk(j)], e_in.at[chunk(i)], e_snd.at[i], e_rcv.at[i], other_y)

    def p_copy(i):
        return remote(p_out.at[chunk(i)], p_in.at[chunk(i)], p_snd.at[i], p_rcv.at[i], above)

    def r_copy(i):
        return remote(r_out.at[chunk(i)], r_in.at[chunk(i)], r_snd.at[i], r_rcv.at[i], other_y)

    def c_copy(i, yy, core):
        j = half_index(i, yy)
        return remote(c_out.at[chunk(j)],
                      prefix.at[state_rows(2 * (i // subs) + yy, core, i % subs)],
                      c_snd.at[j], c_rcv.at[j], other_core)

    def d_copy(i):
        return remote(d_out.at[chunk(i)], d_in.at[chunk(i)], d_snd.at[i], d_rcv.at[i], below)

    def half_index(i, yy):
        return (2 * (i // subs) + yy) * subs + i % subs

    def send_chip(piece):
        for sub in range(subs):
            j = piece * subs + sub
            x_copy(piece, sub).wait_recv()
            chip[chunk(j), :] = total[state_rows(piece, c, sub), :] + x_in[chunk(j), :]

            @pl.when(piece % 2 != y)
            def _():
                e_copy((piece // 2) * subs + sub).start()

    def states(step, _):
        piece = piece_at(step)
        fetch(k_hbm, k_buf, k_sem, piece).wait()
        fetch(v_hbm, v_buf, v_sem, piece).wait()
        for a in range(heads):
            head = piece * heads + a
            cols = pl.ds(pl.multiple_of(head * DH, DH), DH)
            feat = silu_round(k_buf[:, cols])
            k_buf[:, cols] = feat
            vals = v_buf[:, cols]
            parts = [
                lax.dot_general(feat[b * BLK:(b + 1) * BLK], vals[b * BLK:(b + 1) * BLK],
                                (((0,), (0,)), ((), ())), preferred_element_type=F32)
                for b in range(2)
            ]
            first[cols, :] = parts[0]
            total[cols, :] = parts[0] + parts[1]
        @pl.when(step == 0)
        def _():
            pl.semaphore_wait(barrier, neighbours)

        for sub in range(subs):
            x_copy(piece, sub).start()

        @pl.when(step > 0)
        def _():
            send_chip(piece_at(step - 1))

        return 0

    lax.fori_loop(0, steps, states, 0)
    send_chip(piece_at(steps - 1))

    yf = y.astype(F32)
    cf = c.astype(F32)
    causal = (lax.broadcasted_iota(jnp.int32, (BLK, BLK), 0)
              >= lax.broadcasted_iota(jnp.int32, (BLK, BLK), 1))
    count = nz * subs
    lag = (nz - 1 - z) * 4
    behind = BEHIND + SLACK * (nz - 1 - z)

    def heads_of(i, yy):
        piece = 2 * (i // subs) + yy
        if rows < DH:
            return [piece]
        return [(2 * piece + core) * subs + i % subs for core in range(2)]

    def head_cols(head):
        return pl.ds(pl.multiple_of(head * DH, DH), DH)

    def pass_down(i):
        @pl.when((i >= 0) & (i // subs < z))
        def _():
            @pl.when(has_above)
            def _():
                d_copy(i).wait_recv()

            d_out[chunk(i), :] = (d_in[chunk(i), :] + chip[chunk(half_index(i, y)), :]
                                  + e_in[chunk(i), :])
            d_copy(i).start()

    def share(i, yy, base):
        j = half_index(i, yy)
        mine = state_rows(2 * (i // subs) + yy, c, i % subs)
        c_out[chunk(j), :] = base + (1.0 - cf) * total[mine, :]
        c_copy(i, yy, c).start()
        prefix[mine, :] = base + cf * x_in[chunk(j), :]

    def finish(i, yy):
        c_copy(i, yy, 1 - c).wait_recv()
        acc = sumsq[...]
        for head in heads_of(i, yy):
            cols = head_cols(head)
            before = prefix[cols, :]
            carried = [before.astype(BF16), (before + first[cols, :]).astype(BF16)]
            blocks = []
            for b in range(2):
                toks = slice(b * BLK, (b + 1) * BLK)
                left = jnp.concatenate([scores[toks, cols], q_buf[toks, cols]], axis=1)
                right = jnp.concatenate([v_buf[toks, cols], carried[b]], axis=0)
                blocks.append(jnp.dot(left, right, preferred_element_type=F32))
            both = jnp.concatenate(blocks, axis=0)
            mixed[:, cols] = both
            acc = acc + both * both
        sumsq[...] = acc

    def score(i):
        for yy in range(2):
            for head in heads_of(i, yy):
                cols = head_cols(head)
                feat = silu_round(q_buf[:, cols])
                q_buf[:, cols] = feat
                for b in range(2):
                    toks = slice(b * BLK, (b + 1) * BLK)
                    s = lax.dot_general(feat[toks], k_buf[toks, cols],
                                        (((1,), (1,)), ((), ())), preferred_element_type=F32)
                    scores[toks, cols] = jnp.where(causal, s, 0.0).astype(BF16)

    def carry(i, _):
        @pl.when(i < count)
        def _():
            here = chunk(i)
            e_copy(i).wait_recv()

            @pl.when(has_below)
            def _():
                p_copy(i).wait_recv()

            arrived = p_in[here, :]
            sibling = e_in[here, :]
            own = chip[chunk(half_index(i, y)), :]
            p_out[here, :] = arrived + own + sibling

            @pl.when(has_above)
            def _():
                p_copy(i).start()

            r_out[here, :] = arrived + (1.0 - yf) * own
            r_copy(i).start()
            share(i, y, arrived + yf * sibling)

        back = i - behind

        @pl.when((back >= 0) & (back < count))
        def _():
            r_copy(back).wait_recv()
            share(back, 1 - y, r_in[chunk(back), :])

        @pl.when(i - lag < count)
        def _():
            pass_down(i - lag)

        @pl.when(i < count)
        def _():
            @pl.when(i % subs == 0)
            def _():
                for piece in range(2):
                    fetch(q_hbm, q_buf, q_sem, 2 * (i // subs) + piece).wait()
            score(i)

        @pl.when((i >= 1) & (i - 1 < count))
        def _():
            finish(i - 1, y)

        @pl.when(back >= 1)
        def _():
            finish(back - 1, 1 - y)

        return 0

    trips = count + behind + 1
    lax.fori_loop(0, trips, carry, 0)

    def rest_down(i, _):
        @pl.when(i + lag >= trips)
        def _():
            pass_down(i)

        return 0

    lax.fori_loop(0, count, rest_down, 0)

    scale = lax.rsqrt(jnp.sum(sumsq[...], axis=1, keepdims=True) * (1.0 / FEAT) + 1e-05)

    def normalize(step, _):
        cols = pl.ds(pl.multiple_of(step * width, width), width)
        out_ref[:, cols] = (mixed[:, cols] * scale * gain_ref[:, cols]).astype(BF16)
        return 0

    lax.fori_loop(0, steps, normalize, 0)

    for sub in range(subs):
        i = z * subs + sub

        @pl.when(has_above)
        def _():
            d_copy(i).wait_recv()

        fs_ref[sub * grain:(sub + 1) * grain, :] = (
            p_out[chunk(i), :] + d_in[chunk(i), :]) * ((n * q_buf.shape[0]) ** -0.5)

    def drain(i, _):
        for piece in range(2):
            x_copy(2 * (i // subs) + piece, i % subs).wait_send()
            c_copy(i, piece, c).wait_send()
        e_copy(i).wait_send()
        r_copy(i).wait_send()

        @pl.when(has_above)
        def _():
            p_copy(i).wait_send()

        @pl.when(i // subs < z)
        def _():
            d_copy(i).wait_send()

        return 0

    lax.fori_loop(0, count, drain, 0)


def shards(n, query_rows, key_rows, value_rows, out_gain):
    toks = query_rows.shape[0]
    rows = FEAT // n
    grain = min(rows, DH)
    chunks = FEAT // 2 // grain
    steps = n // 2
    full = pltpu.VMEM((FEAT, DH), F32)
    half = pltpu.VMEM((FEAT // 2, DH), F32)
    quarter = pltpu.VMEM((FEAT // 4, DH), F32)
    wide = pltpu.VMEM((toks, FEAT), BF16)
    dma = pltpu.SemaphoreType.DMA
    return pl.pallas_call(
        functools.partial(kernel, n),
        out_shape=(jax.ShapeDtypeStruct((toks, FEAT), BF16),
                   jax.ShapeDtypeStruct((rows, DH), F32)),
        in_specs=[pl.BlockSpec(memory_space=pl.ANY)] * 3
        + [pl.BlockSpec(memory_space=pltpu.VMEM)],
        out_specs=(pl.BlockSpec(memory_space=pltpu.VMEM),
                   pl.BlockSpec(memory_space=pltpu.VMEM)),
        scratch_shapes=[wide] * 4 + [pltpu.VMEM((toks, FEAT), F32), pltpu.VMEM((toks, DH), F32)]
        + [full] * 3 + [half] * 3 + [quarter] * 7
        + [dma((steps,))] * 3 + [dma((chunks,))] * 4 + [dma((chunks // 2,))] * 8,
        compiler_params=pltpu.CompilerParams(
            collective_id=0, has_side_effects=True, vmem_limit_bytes=50 * 1024 * 1024),
        cost_estimate=pl.CostEstimate(
            flops=2 * 4 * toks * FEAT * DH, bytes_accessed=8 * toks * FEAT,
            transcendentals=2 * toks * FEAT),
    )(query_rows, key_rows, value_rows, out_gain.reshape(1, FEAT))


def solution(mesh):
    rows = P(("groups", "ctx"), None)
    return jax.shard_map(
        functools.partial(shards, mesh.shape["ctx"]),
        mesh=mesh,
        in_specs=(rows, rows, rows, P()),
        out_specs=(rows, rows),
        check_vma=False,
    )
```
